32 devices in a mesh: ctx: 8 (over z, x), tp: 4 (over y, core).
Axes of the slice: x: 2, y: 2, z: 4, core: 2. Of those that a mesh axis runs over, the one named last changes fastest.
Arguments:
- pre_gate: bfloat16 [512, 4096], P('ctx', 'tp'), may hold values from -6 to 6
- post_gate: bfloat16 [512, 4096], P('ctx', 'tp'), may hold values from -6 to 6
- features: bfloat16 [512, 4096], P('ctx', 'tp'), may hold values from -6 to 6
- decay_rates: float32 [16, 4096], P(None, 'tp'), may hold values from 0 to 1, as said below
- residues: float32 [16, 4096], P(None, 'tp'), may hold values from -1 to 1
- skip_gain: float32 [4096], P('tp'), may hold values from 0.1 to 1.9
- queries: bfloat16 [512, 4096], P('ctx', 'tp'), may hold values from -20 to 20
- key_rows: bfloat16 [512, 4096], P('ctx', 'tp'), may hold values from -20 to 20
Outputs:
- filtered: bfloat16 [512, 4096], P('ctx', 'tp')
- attended: bfloat16 [512, 4096], P('ctx', 'tp')
The draws below stay inside these ranges and needn't reach their ends.
Inputs may be any that keep to these rules, and one draw needn't show every extreme that they name: `decay_rates`: positive rates.
All inputs are finite; a program needn't handle non-finite values.
Results may differ from the reference program's by a relative error of at most 0.0065.
Values may be sent and summed in bfloat16 or wider, within the bound.
A program may use at most 128 MiB of HBM per device.

```python
import jax
import jax.numpy as jnp
from jax import lax

HEADS = 32
HEAD_SIZE = 128
MODES = 16
CH = 4096
TOKENS = 512


def mode_rates(key, slow_share):
    slow_key, fast_key, pick_key = jax.random.split(key, 3)
    slow_rates = jax.random.uniform(slow_key, (MODES, CH), jnp.float32, jnp.log(0.1 / TOKENS), jnp.log(2.0 / TOKENS))
    fast_rates = jax.random.uniform(fast_key, (MODES, CH), jnp.float32, jnp.log(0.06), jnp.log(0.3))
    chosen = jax.random.uniform(pick_key, (1, CH), jnp.float32) < slow_share
    return jnp.exp(jnp.where(chosen, slow_rates, fast_rates))


def draw_decay_rates(key, part):
    slow_share = 0.5
    return mode_rates(key, slow_share)


def draw_residues(key, part):
    slow_share = 0.5
    rates = mode_rates(key, slow_share)
    key = jax.random.fold_in(key, 11)
    draws_normal = jnp.clip(jax.random.normal(key, (MODES, CH), jnp.float32), -4.0, 4.0)
    values = draws_normal * jnp.sqrt(1.0 - jnp.exp(-2.0 * rates)) / jnp.sqrt(1.0 * MODES)
    return jnp.clip(values, -1.0, 1.0)


def draw_queries(key, part):
    key = jax.random.fold_in(key, 21)
    base_rows = jnp.clip(jax.random.normal(key, (TOKENS, CH), jnp.float32), -4.0, 4.0)
    return base_rows.astype(jnp.bfloat16)


def draw_key_rows(key, part):
    key = jax.random.fold_in(key, 31)
    base_rows = jnp.clip(jax.random.normal(key, (TOKENS, CH), jnp.float32), -4.0, 4.0)
    return base_rows.astype(jnp.bfloat16)


def level_of(rng, shape, shards, smallest, high):
    gain = 1.0
    for dim, parts in shards:
        steps = jax.random.uniform(jax.random.fold_in(jax.random.fold_in(rng, 6), dim), (parts,), jnp.float32, smallest / len(shards), high / len(shards))
        gain = gain * jnp.repeat(jnp.exp(steps), shape[dim] // parts).reshape((-1,) + (1,) * (len(shape) - 1 - dim))
    return gain


def normal_values(rng, shape, deviation, most, cuts=(), kind=jnp.bfloat16):
    drawn = deviation * jax.random.normal(rng, shape, jnp.float32)
    if cuts:
        drawn = drawn * level_of(rng, shape, cuts, -0.22, 0.18)
    return jnp.clip(drawn, -most, most).astype(kind)


def setup_inputs(seed: int = 0) -> dict:
    seeds = jax.random.split(jax.random.key(seed), 9)
    return {
        "pre_gate": normal_values(seeds[0], (TOKENS, CH), 1.0, 6.0, ((0, 8), (1, 4))),
        "post_gate": normal_values(seeds[1], (TOKENS, CH), 1.0, 6.0, ((0, 8), (1, 4))),
        "features": normal_values(seeds[2], (TOKENS, CH), 1.0, 6.0, ((0, 8), (1, 4))),
        "decay_rates": draw_decay_rates(jax.random.fold_in(seeds[8], 71), 0),
        "residues": draw_residues(jax.random.fold_in(seeds[8], 71), 0),
        "skip_gain": jnp.clip(1.0 + 0.18 * jax.random.normal(seeds[5], (CH,), jnp.float32), 0.1, 1.9),
        "queries": draw_queries(jax.random.fold_in(seeds[8], 71), 0),
        "key_rows": draw_key_rows(jax.random.fold_in(seeds[8], 71), 0),
    }


def reference(pre_gate, post_gate, features, decay_rates, residues, skip_gain, queries, key_rows):
    product = pre_gate.astype(jnp.float32) * features.astype(jnp.float32)
    driven = lax.optimization_barrier(product.astype(jnp.bfloat16)).astype(jnp.float32)
    factor = jnp.exp(-decay_rates)

    def advance(state_sum, entry):
        state_sum = factor * state_sum + entry[None, :]
        return state_sum, jnp.sum(residues * state_sum, axis=0)

    _, convolved = lax.scan(advance, jnp.zeros((MODES, CH), jnp.float32), driven)
    convolved = convolved + skip_gain[None, :] * driven
    filtered = (post_gate.astype(jnp.float32) * convolved).astype(jnp.bfloat16)

    scale = HEAD_SIZE ** -0.5

    def split_heads(array):
        return array.astype(jnp.float32).reshape(TOKENS, HEADS, HEAD_SIZE).transpose(1, 0, 2)

    positions = jnp.arange(TOKENS)
    causal = positions[None, :] <= positions[:, None]

    def one_head(triple):
        query_head, key_head, value_head = triple
        scores = jnp.dot(query_head, key_head.T, precision=lax.Precision.HIGHEST) * scale
        scores = jnp.where(causal, scores, -jnp.inf)
        weights = jnp.exp(scores - jnp.max(scores, axis=1, keepdims=True))
        total = jnp.sum(weights, axis=1, keepdims=True)
        rounded = lax.optimization_barrier(weights.astype(jnp.bfloat16)).astype(jnp.float32)
        return jnp.dot(rounded, value_head, precision=lax.Precision.HIGHEST) / total

    attended = lax.map(one_head, (split_heads(queries), split_heads(key_rows), split_heads(filtered)))
    attended = attended.transpose(1, 0, 2).reshape(TOKENS, CH).astype(jnp.bfloat16)
    return filtered, attended
```

```python
import jax
import jax.numpy as jnp
from jax import lax
from jax.experimental import pallas as pl
from jax.experimental.pallas import tpu as pltpu
from jax.sharding import PartitionSpec as P

HEAD_SIZE = 128


very_low = -1e30


def shifted_2(x, axis, by):
    peers = lax.axis_size(axis)
    pairs = [(i, i + by) for i in range(peers) if 0 <= i + by < peers]
    return lax.ppermute(x, axis, pairs)


def toeplitz_local(response, driven):
    tok_rows, chan_width = driven.shape
    block_width = min(128, chan_width)
    block_count = chan_width // block_width
    row_index = jnp.arange(tok_rows)
    lag_index = row_index[:, None] - row_index[None, :]
    shift_table = (lag_index[:, :, None] == row_index[None, None, :]).astype(jnp.float32)
    resp_blocks = response.reshape(tok_rows, block_count, block_width).transpose(1, 0, 2)
    drive_blocks = driven.reshape(tok_rows, block_count, block_width).transpose(1, 0, 2)

    def one_block(block_pair):
        resp_block, drive_block = block_pair
        toeplitz = jnp.einsum(
            "tsl,lc->tsc", shift_table, resp_block, precision=lax.Precision.HIGHEST
        )
        return jnp.einsum("tsc,sc->tc", toeplitz, drive_block, precision=lax.Precision.HIGHEST)

    out_blocks = lax.map(one_block, (resp_blocks, drive_blocks))
    return out_blocks.transpose(1, 0, 2).reshape(tok_rows, chan_width)


def on_device(pre_gate, post_gate, features, decay_rates, residues, skip_gain, queries, key_rows):
    tok_rows, chan_width = pre_gate.shape
    product = pre_gate.astype(jnp.float32) * features.astype(jnp.float32)
    driven = lax.optimization_barrier(product.astype(jnp.bfloat16)).astype(jnp.float32)
    offsets = jnp.arange(tok_rows, dtype=jnp.float32)
    powers = jnp.exp(-decay_rates[None, :, :] * offsets[:, None, None])
    response = jnp.einsum("tmc,mc->tc", powers, residues, precision=lax.Precision.HIGHEST)
    local_part = toeplitz_local(response, driven)
    own_state = jnp.einsum("smc,sc->mc", powers[::-1], driven, precision=lax.Precision.HIGHEST)
    block_decay = jnp.exp(-decay_rates * tok_rows)

    def relay_step(turn_index, state_sum):
        return shifted_2(
            (block_decay * state_sum + own_state).astype(jnp.bfloat16), "ctx", 1
        ).astype(jnp.float32)

    incoming = lax.fori_loop(0, lax.axis_size("ctx") - 1, relay_step, jnp.zeros_like(own_state))
    shifted = powers * jnp.exp(-decay_rates)[None, :, :]
    cross_part = jnp.einsum(
        "tmc,mc->tc", shifted, residues * incoming, precision=lax.Precision.HIGHEST
    )
    convolved = local_part + cross_part + skip_gain[None, :] * driven
    filtered = (post_gate.astype(jnp.float32) * convolved).astype(jnp.bfloat16)
    head_count = chan_width // HEAD_SIZE
    scale = HEAD_SIZE ** (-0.5)
    query_heads = queries.reshape(tok_rows, head_count, HEAD_SIZE)
    query_pos = lax.axis_index("ctx") * tok_rows + jnp.arange(tok_rows)
    start_max = jnp.full((head_count, tok_rows), very_low, jnp.float32)
    key_piece = lax.all_gather(key_rows, "ctx", axis=0, tiled=True)
    value_piece = lax.all_gather(filtered, "ctx", axis=0, tiled=True)
    piece_rows = key_piece.shape[0]
    key_heads = key_piece.reshape(piece_rows, head_count, HEAD_SIZE)
    scores = (
        jnp.einsum("qhe,khe->hqk", query_heads, key_heads, preferred_element_type=jnp.float32)
        * scale
    )
    key_pos = jnp.arange(piece_rows)
    allowed = key_pos[None, :] <= query_pos[:, None]
    scores, allowed = (jnp.where(allowed[None], scores, very_low), allowed)
    new_max = jnp.maximum(start_max, jnp.max(scores, axis=-1))
    weights = jnp.where(allowed[None], jnp.exp(scores - new_max[..., None]), 0.0)
    new_sum = jnp.sum(weights, axis=-1)
    piece_rows = value_piece.shape[0]
    value_heads = value_piece.reshape(piece_rows, head_count, HEAD_SIZE)
    new_acc = jnp.einsum(
        "hqk,khe->hqe",
        weights.astype(jnp.bfloat16),
        value_heads,
        preferred_element_type=jnp.float32,
    )
    attended = (
        (new_acc / new_sum[..., None])
        .transpose(1, 0, 2)
        .reshape(tok_rows, chan_width)
        .astype(jnp.bfloat16)
    )
    return (filtered, attended)


MESH = pl.DeviceIdType.MESH
QK, STATE, PREFIX, VALUE, OUT = range(5)


def mixer_kernel(
    pre_ref, post_ref, feat_ref, decay_ref, resid_ref, skip_ref, q_ref, k_ref,
    filt_ref, att_ref,
    qk_send, qk_all, st_send, st_all, pf_send, pf_all, v_send, v_all, att_send, att_all,
    driven, conv, factor, gain, state, jump, weights, totals,
    send_sems, recv_sems,
):
    heads, rows, size = v_send.shape
    modes = decay_ref.shape[0]
    me = lax.axis_index("ctx")

    barrier = pltpu.get_barrier_semaphore()
    for d in range(1, heads):
        pl.semaphore_signal(
            barrier, inc=1, device_id={"ctx": lax.rem(me + d, heads)}, device_id_type=MESH
        )

    def exchange(phase, src, dst):
        copies = []
        for d in range(1, heads):
            peer = lax.rem(me + d, heads)
            copy = pltpu.make_async_remote_copy(
                src_ref=src.at[peer],
                dst_ref=dst.at[me],
                send_sem=send_sems.at[phase, d],
                recv_sem=recv_sems.at[phase, d],
                device_id={"ctx": peer},
                device_id_type=MESH,
            )
            copy.start()
            copies.append(copy)
        dst[me] = src[me]
        return copies

    for h in range(heads):
        lanes = slice(h * size, (h + 1) * size)
        product = pre_ref[:, lanes].astype(jnp.float32) * feat_ref[:, lanes].astype(jnp.float32)
        driven[h * rows:(h + 1) * rows] = product.astype(jnp.bfloat16).astype(jnp.float32)
        decay = decay_ref[:, lanes]
        factor[h * modes:(h + 1) * modes] = jnp.exp(-decay)
        jump[h * modes:(h + 1) * modes] = jnp.exp(-decay * rows)
        gain[h * modes:(h + 1) * modes] = resid_ref[:, lanes]

    def by_mode(ref):
        return [ref[pl.ds(m, heads, stride=modes), :] for m in range(modes)]

    f = by_mode(factor)
    step = 8

    def end_state(turn, s):
        for u in range(step):
            d = driven[pl.ds(turn * step + u, heads, stride=rows), :]
            s = [f[m] * s[m] + d for m in range(modes)]
        return s

    zero = [jnp.zeros((heads, size), jnp.float32)] * modes
    ended = lax.fori_loop(0, rows // step, end_state, zero)
    for m in range(modes):
        state[pl.ds(m, heads, stride=modes), :] = ended[m]
    for h in range(heads):
        st_send[h] = state[h * modes:(h + 1) * modes].astype(jnp.bfloat16)

    pl.semaphore_wait(barrier, heads - 1)
    st_copies = exchange(STATE, st_send, st_all)
    for h in range(heads):
        lanes = slice(h * size, (h + 1) * size)
        qk_send[h, 0] = q_ref[:, lanes]
        qk_send[h, 1] = k_ref[:, lanes]
    qk_copies = exchange(QK, qk_send, qk_all)

    for copy in st_copies:
        copy.wait_recv()
    leap = jump[pl.ds(pl.multiple_of(me * modes, modes), modes), :]
    running = jnp.zeros((modes, size), jnp.float32)
    for c in range(heads):
        pf_send[c] = running.astype(jnp.bfloat16)
        running = leap * running + st_all[c].astype(jnp.float32)
    pf_copies = exchange(PREFIX, pf_send, pf_all)
    for copy in pf_copies:
        copy.wait_recv()
    for h in range(heads):
        state[h * modes:(h + 1) * modes] = pf_all[h].astype(jnp.float32)

    g = by_mode(gain)
    skip = skip_ref[...]

    def filter_rows(turn, s):
        for u in range(step):
            at = pl.ds(turn * step + u, heads, stride=rows)
            d = driven[at, :]
            s = [f[m] * s[m] + d for m in range(modes)]
            terms = [g[m] * s[m] for m in range(modes)] + [skip * d]
            while len(terms) > 1:
                terms = [sum(terms[i + 1:i + 2], terms[i]) for i in range(0, len(terms), 2)]
            conv[at, :] = terms[0]
        return s

    lax.fori_loop(0, rows // step, filter_rows, by_mode(state))
    for h in range(heads):
        lanes = slice(h * size, (h + 1) * size)
        gated = post_ref[:, lanes].astype(jnp.float32) * conv[h * rows:(h + 1) * rows]
        gated = gated.astype(jnp.bfloat16)
        filt_ref[:, lanes] = gated
        v_send[h] = gated
    v_copies = exchange(VALUE, v_send, v_all)

    for copy in qk_copies:
        copy.wait_recv()
    pair = 2
    tall = pair * rows
    scale = size ** -0.5
    blocks = heads // pair
    for b in range(blocks):
        wide = (b + 1) * tall
        q = qk_all[b * pair:(b + 1) * pair, 0].reshape(tall, size)
        k = qk_all[0:(b + 1) * pair, 1].reshape(wide, size)
        score = lax.dot_general(
            q, k, (((1,), (1,)), ((), ())), preferred_element_type=jnp.float32
        ) * scale
        row = lax.broadcasted_iota(jnp.int32, (tall, wide), 0) + b * tall
        column = lax.broadcasted_iota(jnp.int32, (tall, wide), 1)
        score = jnp.where(column <= row, score, very_low)
        weight = jnp.exp(score - jnp.max(score, axis=1, keepdims=True))
        totals[b * tall:(b + 1) * tall] = jnp.broadcast_to(
            jnp.sum(weight, axis=1, keepdims=True), (tall, size)
        )
        weights[b * tall:(b + 1) * tall, 0:wide] = weight.astype(jnp.bfloat16)

    for copy in v_copies:
        copy.wait_recv()
    for b in range(blocks):
        wide = (b + 1) * tall
        v = v_all[0:(b + 1) * pair].reshape(wide, size)
        acc = jnp.dot(
            weights[b * tall:(b + 1) * tall, 0:wide], v, preferred_element_type=jnp.float32
        )
        out = (acc / totals[b * tall:(b + 1) * tall]).astype(jnp.bfloat16)
        att_send[b * pair:(b + 1) * pair] = out.reshape(pair, rows, size)
    att_copies = exchange(OUT, att_send, att_all)
    for copy in att_copies:
        copy.wait_recv()
    for h in range(heads):
        att_ref[:, h * size:(h + 1) * size] = att_all[h]
    for copy in st_copies + qk_copies + pf_copies + v_copies + att_copies:
        copy.wait_send()


def by_heads(pre_gate, post_gate, features, decay_rates, residues, skip_gain, queries, key_rows):
    rows, width = pre_gate.shape
    modes = decay_rates.shape[0]
    size = HEAD_SIZE
    heads = width // size
    shape = jax.ShapeDtypeStruct((rows, width), jnp.bfloat16)
    bf16 = lambda *dims: pltpu.VMEM(dims, jnp.bfloat16)
    f32 = lambda *dims: pltpu.VMEM(dims, jnp.float32)
    small = [bf16(heads, modes, size)] * 4
    blocks = [bf16(heads, rows, size)] * 4
    return tuple(pl.pallas_call(
        mixer_kernel,
        out_shape=(shape, shape),
        in_specs=[pl.BlockSpec(memory_space=pltpu.VMEM)] * 8,
        out_specs=(pl.BlockSpec(memory_space=pltpu.VMEM),) * 2,
        scratch_shapes=[
            bf16(heads, 2, rows, size), bf16(heads, 2, rows, size),
            *small, *blocks,
            f32(heads * rows, size), f32(heads * rows, size),
            *[f32(heads * modes, size)] * 4,
            bf16(heads * rows, heads * rows), f32(heads * rows, size),
            pltpu.SemaphoreType.DMA((5, heads)),
            pltpu.SemaphoreType.DMA((5, heads)),
        ],
        compiler_params=pltpu.CompilerParams(
            collective_id=0, has_side_effects=True, vmem_limit_bytes=32 * 1024 * 1024
        ),
    )(
        pre_gate, post_gate, features, decay_rates, residues,
        skip_gain.reshape(heads, size), queries, key_rows,
    ))


def pick_body(*args):
    rows, width = args[0].shape
    whole_heads = lax.axis_size("ctx") * HEAD_SIZE == width
    return (by_heads if whole_heads and rows % 16 == 0 else on_device)(*args)


def solution(mesh):
    placed = (
        P("ctx", "tp"),
        P("ctx", "tp"),
        P("ctx", "tp"),
        P(None, "tp"),
        P(None, "tp"),
        P("tp"),
        P("ctx", "tp"),
        P("ctx", "tp"),
    )
    return jax.shard_map(
        pick_body,
        mesh=mesh,
        in_specs=placed,
        out_specs=(P("ctx", "tp"), P("ctx", "tp")),
        check_vma=False,
    )
```

```python
import jax
import jax.numpy as jnp
from jax import lax
from jax.experimental import pallas as pl
from jax.experimental.pallas import tpu as pltpu
from jax.sharding import PartitionSpec as P

HEAD_SIZE = 128


very_low = -1e30


def shifted_2(x, axis, by):
    peers = lax.axis_size(axis)
    pairs = [(i, i + by) for i in range(peers) if 0 <= i + by < peers]
    return lax.ppermute(x, axis, pairs)


def toeplitz_local(response, driven):
    tok_rows, chan_width = driven.shape
    block_width = min(128, chan_width)
    block_count = chan_width // block_width
    row_index = jnp.arange(tok_rows)
    lag_index = row_index[:, None] - row_index[None, :]
    shift_table = (lag_index[:, :, None] == row_index[None, None, :]).astype(jnp.float32)
    resp_blocks = response.reshape(tok_rows, block_count, block_width).transpose(1, 0, 2)
    drive_blocks = driven.reshape(tok_rows, block_count, block_width).transpose(1, 0, 2)

    def one_block(block_pair):
        resp_block, drive_block = block_pair
        toeplitz = jnp.einsum(
            "tsl,lc->tsc", shift_table, resp_block, precision=lax.Precision.HIGHEST
        )
        return jnp.einsum("tsc,sc->tc", toeplitz, drive_block, precision=lax.Precision.HIGHEST)

    out_blocks = lax.map(one_block, (resp_blocks, drive_blocks))
    return out_blocks.transpose(1, 0, 2).reshape(tok_rows, chan_width)


def on_device(pre_gate, post_gate, features, decay_rates, residues, skip_gain, queries, key_rows):
    tok_rows, chan_width = pre_gate.shape
    product = pre_gate.astype(jnp.float32) * features.astype(jnp.float32)
    driven = lax.optimization_barrier(product.astype(jnp.bfloat16)).astype(jnp.float32)
    offsets = jnp.arange(tok_rows, dtype=jnp.float32)
    powers = jnp.exp(-decay_rates[None, :, :] * offsets[:, None, None])
    response = jnp.einsum("tmc,mc->tc", powers, residues, precision=lax.Precision.HIGHEST)
    local_part = toeplitz_local(response, driven)
    own_state = jnp.einsum("smc,sc->mc", powers[::-1], driven, precision=lax.Precision.HIGHEST)
    block_decay = jnp.exp(-decay_rates * tok_rows)

    def relay_step(turn_index, state_sum):
        return shifted_2(
            (block_decay * state_sum + own_state).astype(jnp.bfloat16), "ctx", 1
        ).astype(jnp.float32)

    incoming = lax.fori_loop(0, lax.axis_size("ctx") - 1, relay_step, jnp.zeros_like(own_state))
    shifted = powers * jnp.exp(-decay_rates)[None, :, :]
    cross_part = jnp.einsum(
        "tmc,mc->tc", shifted, residues * incoming, precision=lax.Precision.HIGHEST
    )
    convolved = local_part + cross_part + skip_gain[None, :] * driven
    filtered = (post_gate.astype(jnp.float32) * convolved).astype(jnp.bfloat16)
    head_count = chan_width // HEAD_SIZE
    scale = HEAD_SIZE ** (-0.5)
    query_heads = queries.reshape(tok_rows, head_count, HEAD_SIZE)
    query_pos = lax.axis_index("ctx") * tok_rows + jnp.arange(tok_rows)
    start_max = jnp.full((head_count, tok_rows), very_low, jnp.float32)
    key_piece = lax.all_gather(key_rows, "ctx", axis=0, tiled=True)
    value_piece = lax.all_gather(filtered, "ctx", axis=0, tiled=True)
    piece_rows = key_piece.shape[0]
    key_heads = key_piece.reshape(piece_rows, head_count, HEAD_SIZE)
    scores = (
        jnp.einsum("qhe,khe->hqk", query_heads, key_heads, preferred_element_type=jnp.float32)
        * scale
    )
    key_pos = jnp.arange(piece_rows)
    allowed = key_pos[None, :] <= query_pos[:, None]
    scores, allowed = (jnp.where(allowed[None], scores, very_low), allowed)
    new_max = jnp.maximum(start_max, jnp.max(scores, axis=-1))
    weights = jnp.where(allowed[None], jnp.exp(scores - new_max[..., None]), 0.0)
    new_sum = jnp.sum(weights, axis=-1)
    piece_rows = value_piece.shape[0]
    value_heads = value_piece.reshape(piece_rows, head_count, HEAD_SIZE)
    new_acc = jnp.einsum(
        "hqk,khe->hqe",
        weights.astype(jnp.bfloat16),
        value_heads,
        preferred_element_type=jnp.float32,
    )
    attended = (
        (new_acc / new_sum[..., None])
        .transpose(1, 0, 2)
        .reshape(tok_rows, chan_width)
        .astype(jnp.bfloat16)
    )
    return (filtered, attended)


MESH = pl.DeviceIdType.MESH
QK, STATE, PREFIX, VALUE, OUT = range(5)


def total_of(terms):
    while len(terms) > 1:
        terms = [sum(terms[i + 1:i + 2], terms[i]) for i in range(0, len(terms), 2)]
    return terms[0]


def mixer_kernel(
    pre_hbm, feat_hbm, decay_hbm, resid_hbm, skip_hbm, q_hbm, k_hbm, post_hbm,
    filt_ref, att_ref,
    pre_ref, feat_ref, decay_ref, resid_ref, skip_ref, q_ref, k_ref, post_ref,
    qk_send, qk_all, st_send, st_all, pf_send, pf_all, v_send, v_all, att_send, att_all,
    driven, conv, factor, gain, state, jump, weights, totals,
    send_sems, recv_sems, load_sems,
):
    sources = (pre_hbm, feat_hbm, decay_hbm, resid_hbm, skip_hbm, q_hbm, k_hbm, post_hbm)
    places = (pre_ref, feat_ref, decay_ref, resid_ref, skip_ref, q_ref, k_ref, post_ref)
    loads = [
        pltpu.make_async_copy(source, place, load_sems.at[i])
        for i, (source, place) in enumerate(zip(sources, places))
    ]
    for load in loads:
        load.start()
    heads, rows, size = v_send.shape
    modes = decay_ref.shape[0]
    me = lax.axis_index("ctx")

    barrier = pltpu.get_barrier_semaphore()
    for d in range(1, heads):
        pl.semaphore_signal(
            barrier, inc=1, device_id={"ctx": lax.rem(me + d, heads)}, device_id_type=MESH
        )

    def exchange(phase, src, dst):
        copies = []
        for d in range(1, heads):
            peer = lax.rem(me + d, heads)
            copy = pltpu.make_async_remote_copy(
                src_ref=src.at[peer],
                dst_ref=dst.at[me],
                send_sem=send_sems.at[phase, d],
                recv_sem=recv_sems.at[phase, d],
                device_id={"ctx": peer},
                device_id_type=MESH,
            )
            copy.start()
            copies.append(copy)
        dst[me] = src[me]
        return copies

    for load in loads[:5]:
        load.wait()
    for h in range(heads):
        lanes = slice(h * size, (h + 1) * size)
        product = pre_ref[:, lanes].astype(jnp.float32) * feat_ref[:, lanes].astype(jnp.float32)
        driven[h * rows:(h + 1) * rows] = product.astype(jnp.bfloat16).astype(jnp.float32)
        decay = decay_ref[:, lanes]
        factor[h * modes:(h + 1) * modes] = jnp.exp(-decay)
        jump[h * modes:(h + 1) * modes] = jnp.exp(-decay * rows)
        gain[h * modes:(h + 1) * modes] = resid_ref[:, lanes]

    def by_mode(ref):
        return [ref[pl.ds(m, heads, stride=modes), :] for m in range(modes)]

    f = by_mode(factor)
    step = 8

    def end_state(turn, s):
        for u in range(step):
            d = driven[pl.ds(turn * step + u, heads, stride=rows), :]
            s = [f[m] * s[m] + d for m in range(modes)]
        return s

    zero = [jnp.zeros((heads, size), jnp.float32)] * modes
    ended = lax.fori_loop(0, rows // step, end_state, zero)
    for m in range(modes):
        state[pl.ds(m, heads, stride=modes), :] = ended[m]
    for h in range(heads):
        st_send[h] = state[h * modes:(h + 1) * modes].astype(jnp.bfloat16)

    pl.semaphore_wait(barrier, heads - 1)
    st_copies = exchange(STATE, st_send, st_all)
    for load in loads[5:]:
        load.wait()
    for h in range(heads):
        lanes = slice(h * size, (h + 1) * size)
        qk_send[h, 0] = q_ref[:, lanes]
        qk_send[h, 1] = k_ref[:, lanes]
    qk_copies = exchange(QK, qk_send, qk_all)

    g = by_mode(gain)
    skip = skip_ref[...]

    def filter_rows(turn, s):
        for u in range(step):
            at = pl.ds(turn * step + u, heads, stride=rows)
            d = driven[at, :]
            s = [f[m] * s[m] + d for m in range(modes)]
            terms = [g[m] * s[m] for m in range(modes)] + [skip * d]
            conv[at, :] = total_of(terms)
        return s

    lax.fori_loop(0, rows // step, filter_rows, zero)

    for copy in st_copies:
        copy.wait_recv()
    leap = jump[pl.ds(pl.multiple_of(me * modes, modes), modes), :]
    running = jnp.zeros((modes, size), jnp.float32)
    for c in range(heads):
        pf_send[c] = running.astype(jnp.bfloat16)
        running = leap * running + st_all[c].astype(jnp.float32)
    pf_copies = exchange(PREFIX, pf_send, pf_all)
    for copy in pf_copies:
        copy.wait_recv()
    for h in range(heads):
        state[h * modes:(h + 1) * modes] = pf_all[h].astype(jnp.float32)

    def add_incoming(turn, s):
        for u in range(step):
            at = pl.ds(turn * step + u, heads, stride=rows)
            s = [f[m] * s[m] for m in range(modes)]
            conv[at, :] += total_of(s)
        return s

    start = [g[m] * s for m, s in enumerate(by_mode(state))]
    lax.fori_loop(0, rows // step, add_incoming, start)
    for h in range(heads):
        lanes = slice(h * size, (h + 1) * size)
        gated = post_ref[:, lanes].astype(jnp.float32) * conv[h * rows:(h + 1) * rows]
        gated = gated.astype(jnp.bfloat16)
        filt_ref[:, lanes] = gated
        v_send[h] = gated
    v_copies = exchange(VALUE, v_send, v_all)

    for copy in qk_copies:
        copy.wait_recv()
    pair = 2
    tall = pair * rows
    scale = size ** -0.5
    blocks = heads // pair
    for b in range(blocks):
        wide = (b + 1) * tall
        q = qk_all[b * pair:(b + 1) * pair, 0].reshape(tall, size)
        k = qk_all[0:(b + 1) * pair, 1].reshape(wide, size)
        score = lax.dot_general(
            q, k, (((1,), (1,)), ((), ())), preferred_element_type=jnp.float32
        ) * scale
        row = lax.broadcasted_iota(jnp.int32, (tall, wide), 0) + b * tall
        column = lax.broadcasted_iota(jnp.int32, (tall, wide), 1)
        score = jnp.where(column <= row, score, very_low)
        weight = jnp.exp(score - jnp.max(score, axis=1, keepdims=True))
        totals[b * tall:(b + 1) * tall] = jnp.broadcast_to(
            jnp.sum(weight, axis=1, keepdims=True), (tall, size)
        )
        weights[b * tall:(b + 1) * tall, 0:wide] = weight.astype(jnp.bfloat16)

    for copy in v_copies:
        copy.wait_recv()
    for b in range(blocks):
        wide = (b + 1) * tall
        v = v_all[0:(b + 1) * pair].reshape(wide, size)
        acc = jnp.dot(
            weights[b * tall:(b + 1) * tall, 0:wide], v, preferred_element_type=jnp.float32
        )
        out = (acc / totals[b * tall:(b + 1) * tall]).astype(jnp.bfloat16)
        att_send[b * pair:(b + 1) * pair] = out.reshape(pair, rows, size)
    att_copies = exchange(OUT, att_send, att_all)
    for copy in att_copies:
        copy.wait_recv()
    for h in range(heads):
        att_ref[:, h * size:(h + 1) * size] = att_all[h]
    for copy in st_copies + qk_copies + pf_copies + v_copies + att_copies:
        copy.wait_send()


def by_heads(pre_gate, post_gate, features, decay_rates, residues, skip_gain, queries, key_rows):
    rows, width = pre_gate.shape
    modes = decay_rates.shape[0]
    size = HEAD_SIZE
    heads = width // size
    shape = jax.ShapeDtypeStruct((rows, width), jnp.bfloat16)
    bf16 = lambda *dims: pltpu.VMEM(dims, jnp.bfloat16)
    f32 = lambda *dims: pltpu.VMEM(dims, jnp.float32)
    small = [bf16(heads, modes, size)] * 4
    blocks = [bf16(heads, rows, size)] * 4
    return tuple(pl.pallas_call(
        mixer_kernel,
        out_shape=(shape, shape),
        in_specs=[pl.BlockSpec(memory_space=pltpu.HBM)] * 8,
        out_specs=(pl.BlockSpec(memory_space=pltpu.VMEM),) * 2,
        scratch_shapes=[
            bf16(rows, width), bf16(rows, width), f32(modes, width), f32(modes, width),
            f32(heads, size), bf16(rows, width), bf16(rows, width), bf16(rows, width),
            bf16(heads, 2, rows, size), bf16(heads, 2, rows, size),
            *small, *blocks,
            f32(heads * rows, size), f32(heads * rows, size),
            *[f32(heads * modes, size)] * 4,
            bf16(heads * rows, heads * rows), f32(heads * rows, size),
            pltpu.SemaphoreType.DMA((5, heads)),
            pltpu.SemaphoreType.DMA((5, heads)),
            pltpu.SemaphoreType.DMA((8,)),
        ],
        compiler_params=pltpu.CompilerParams(
            collective_id=0, has_side_effects=True, vmem_limit_bytes=60 * 1024 * 1024
        ),
    )(
        pre_gate, features, decay_rates, residues, skip_gain.reshape(heads, size),
        queries, key_rows, post_gate,
    ))


def pick_body(*args):
    rows, width = args[0].shape
    whole_heads = lax.axis_size("ctx") * HEAD_SIZE == width
    return (by_heads if whole_heads and rows % 16 == 0 else on_device)(*args)


def solution(mesh):
    placed = (
        P("ctx", "tp"),
        P("ctx", "tp"),
        P("ctx", "tp"),
        P(None, "tp"),
        P(None, "tp"),
        P("tp"),
        P("ctx", "tp"),
        P("ctx", "tp"),
    )
    return jax.shard_map(
        pick_body,
        mesh=mesh,
        in_specs=placed,
        out_specs=(P("ctx", "tp"), P("ctx", "tp")),
        check_vma=False,
    )
```
